256 devices in a mesh: sta: 64 (over y, z_hi, x), win: 4 (over z_lo, core).
Axes of the slice: x: 4, y: 4, z: 8 (z_hi: 4, z_lo: 2; z = z_hi * 2 + z_lo), core: 2. Of those that a mesh axis runs over, the one named last changes fastest.
Arguments:
- records: bfloat16 [2048, 64, 2048], P('sta', 'win'), may hold values from -160 to 160
- gap_mask: int32 [2048, 64], P('sta', 'win'), may hold values from 0 to 1, as said below
Outputs:
- stacks: bfloat16 [3, 2048, 32, 2001], P(None, ('sta', 'win'))
The draws below stay inside these ranges and needn't reach their ends.
Inputs may be any that keep to these rules, and one draw needn't show every extreme that they name: `gap_mask`: some channels have no valid window at all.
All inputs are finite; a program needn't handle non-finite values.
Results may differ from the reference program's by a relative error of at most 0.014.
Values may be sent and summed in bfloat16 or wider, within the bound.
No kernel may reach another device: no remote copies, remote signals or barrier semaphores. Data moves between devices by JAX's collectives and lax.ppermute only.
A program may use at most 128 MiB of HBM per device.

```python
import math
import jax
import jax.numpy as jnp
from jax import lax

SEG = 2048
NFFT = 4096
BINS = 512
SMOOTH = 4
LAGHALF = 1000
CH = 32
WIN_DEV = 16
ROUNDS = 3
LAGS = 2001
BLOCKS = 64
CHANNELS = 2048
WINDOWS = 64
N_WIN = 4


def draw_records(key, part):
    key = jax.random.fold_in(key, 11)
    keys = jax.random.split(key, 3)
    channel_scale = jnp.exp(jax.random.uniform(keys[0], (CHANNELS, 1, 1), jnp.float32, 0.0, math.log(10.0)))
    window_scale = jnp.exp(jax.random.uniform(keys[1], (CHANNELS, WINDOWS, 1), jnp.float32, math.log(0.5), math.log(2.0)))
    base = jnp.clip(jax.random.normal(keys[2], (CHANNELS, WINDOWS, SEG), jnp.float32), -5.0, 5.0)
    values = base * channel_scale * window_scale
    return jnp.clip(values, -160.0, 160.0).astype(jnp.bfloat16)


def draw_gap_mask(key, part):
    key = jax.random.fold_in(key, 23)
    keys = jax.random.split(key, 3)
    silent = jax.random.randint(keys[0], (CHANNELS, 1), 0, 24) == 0
    chosen = jnp.arange(CHANNELS, dtype=jnp.int32)[:, None] == jax.random.randint(keys[2], (), 0, CHANNELS)
    clean = jax.random.randint(keys[1], (CHANNELS, WINDOWS), 0, 5) > 0
    return jnp.where(silent | chosen, 0, clean.astype(jnp.int32)).astype(jnp.int32)


def setup_inputs(seed: int = 0) -> dict:
    splits = jax.random.split(jax.random.key(seed), 3)
    return {
        "records": draw_records(jax.random.fold_in(splits[2], 71), 0),
        "gap_mask": draw_gap_mask(jax.random.fold_in(splits[2], 71), 0),
    }


def forward_table():
    samples = jnp.arange(SEG, dtype=jnp.int32)
    frequencies = jnp.arange(1, BINS + 1, dtype=jnp.int32)
    phases = samples[:, None] * frequencies[None, :] % NFFT
    angles = phases.astype(jnp.float32) * (2.0 * math.pi / NFFT)
    norm_scale = 1.0 / math.sqrt(SEG)
    return jnp.concatenate([jnp.cos(angles) * norm_scale, -jnp.sin(angles) * norm_scale], axis=1).astype(jnp.bfloat16)

def inverse_table():
    frequencies = jnp.arange(1, BINS + 1, dtype=jnp.int32)
    shifts = jnp.arange(LAGS, dtype=jnp.int32) - LAGHALF
    phases = frequencies[:, None] * shifts[None, :] % NFFT
    angles = phases.astype(jnp.float32) * (2.0 * math.pi / NFFT)
    norm_scale = math.sqrt(2.0 / BINS)
    return jnp.concatenate([jnp.cos(angles) * norm_scale, -jnp.sin(angles) * norm_scale], axis=0).astype(jnp.bfloat16)

def whitened_spectra(records, valid_rows, forward):
    signal = records.astype(jnp.float32)
    centred = signal - lax.optimization_barrier(jnp.mean(signal, axis=-1, keepdims=True))
    spread = jnp.sqrt(lax.optimization_barrier(jnp.mean(centred * centred, axis=-1, keepdims=True)) + 1e-06)
    normal_rows = (centred / spread).astype(jnp.bfloat16)
    row_count, window_count = (records.shape[0], records.shape[1])
    spectrum = jnp.dot(normal_rows.reshape(row_count * window_count, SEG), forward, preferred_element_type=jnp.float32)
    spectrum = spectrum.reshape(row_count, window_count, 2 * BINS)
    real_part = spectrum[..., :BINS]
    imag_part = spectrum[..., BINS:]
    power_sum = real_part * real_part + imag_part * imag_part
    padded = jnp.pad(power_sum, ((0, 0), (0, 0), (SMOOTH, SMOOTH)))
    filled = jnp.pad(jnp.ones((BINS,), jnp.float32), (SMOOTH, SMOOTH))
    window_sum = padded[..., 0:BINS]
    ones_sum = filled[0:BINS]
    for offset in range(1, 2 * SMOOTH + 1):
        window_sum = window_sum + padded[..., offset:offset + BINS]
        ones_sum = ones_sum + filled[offset:offset + BINS]
    smoothed = window_sum / ones_sum
    factor = 1.0 / jnp.sqrt(smoothed + 0.1)
    joined = jnp.concatenate([real_part * factor, imag_part * factor], axis=-1)
    return (joined * valid_rows[..., None]).astype(jnp.bfloat16)

def cross_spectra(own_spec, other_spec):
    own_real = own_spec[..., :BINS].astype(jnp.float32)
    own_imag = own_spec[..., BINS:].astype(jnp.float32)
    right_side = jnp.concatenate([other_spec[..., :BINS], other_spec[..., BINS:]], axis=1).astype(jnp.float32)
    left_real = jnp.concatenate([own_real, own_imag], axis=1)
    left_imag = jnp.concatenate([own_imag, -own_real], axis=1)
    real_sum = jnp.einsum('cwk,qwk->cqk', left_real, right_side)
    imag_sum = jnp.einsum('cwk,qwk->cqk', left_imag, right_side)
    return jnp.concatenate([real_sum, imag_sum], axis=-1)

def finish_pairs(summed, pair_count, inverse):
    row_count, partner_count = (summed.shape[0], summed.shape[1])
    low = summed.astype(jnp.bfloat16).reshape(row_count * partner_count, 2 * BINS)
    lagged = jnp.dot(low, inverse, preferred_element_type=jnp.float32).reshape(row_count, partner_count, LAGS)
    return (lagged / jnp.sqrt(jnp.maximum(pair_count, 1.0))[..., None]).astype(jnp.bfloat16)

def reference(records, gap_mask):
    forward = forward_table()
    inverse = inverse_table()
    valid_rows = gap_mask.astype(jnp.float32)
    block_records = records.reshape(BLOCKS, CH, WINDOWS, SEG)
    block_valid = valid_rows.reshape(BLOCKS, CH, WINDOWS)
    whitened = lax.map(lambda block_pair: whitened_spectra(block_pair[0], block_pair[1], forward), (block_records, block_valid))

    def one_block(block_items):
        own_spec, shifted, own_valid, shifted_valid = block_items
        own_groups = own_spec.reshape(CH, N_WIN, WIN_DEV, 2 * BINS)
        shifted_groups = shifted.reshape(CH, N_WIN, WIN_DEV, 2 * BINS)
        running = jnp.zeros((CH, CH, 2 * BINS), jnp.float32)
        for group_index in range(N_WIN):
            partial_value = cross_spectra(own_groups[:, group_index], shifted_groups[:, group_index])
            running = running + lax.optimization_barrier(partial_value.astype(jnp.bfloat16)).astype(jnp.float32)
        pair_count = jnp.dot(own_valid, shifted_valid.T, preferred_element_type=jnp.float32, precision=lax.Precision.HIGHEST)
        return finish_pairs(running, pair_count, inverse)
    outputs = []
    for round_index in range(ROUNDS):
        shifted = jnp.roll(whitened, round_index + 1, axis=0)
        shifted_valid = jnp.roll(block_valid, round_index + 1, axis=0)
        result = lax.map(one_block, (whitened, shifted, block_valid, shifted_valid))
        outputs.append(result.reshape(CHANNELS, CH, LAGS))
    return jnp.stack(outputs)
```

```python
import functools
import math

import jax
import jax.numpy as jnp
import numpy as np
from jax import lax
from jax.experimental import pallas as pl
from jax.experimental.pallas import tpu as pltpu
from jax.sharding import Mesh, PartitionSpec as P

SEG = 2048
NFFT = 4096
BINS = 512
SMOOTH = 4
LAGHALF = 1000
LAGS = 2001
CH = 32
WIN = 16
BF = jnp.bfloat16
F32 = jnp.float32
PARTS = 1
NB = BINS // 16 // PARTS
PART_ROWS = 8 * NB
MASK_ROW = PARTS * PART_ROWS
SENT_ROWS = MASK_ROW + 8
GROUP = ("x", "zl", "core")
STATIONS = ("y", "zh", "x")


def forward_table():
    phases = np.arange(1, BINS + 1)[:, None] * np.arange(SEG)[None, :] % NFFT
    angles = phases * (2.0 * math.pi / NFFT)
    table = np.concatenate([np.cos(angles), -np.sin(angles)], axis=0) / math.sqrt(SEG)
    return table.astype(np.float32).astype(jnp.bfloat16)


def inverse_table():
    phases = np.arange(1, BINS + 1)[:, None] * (np.arange(LAGS) - LAGHALF)[None, :] % NFFT
    angles = phases * (2.0 * math.pi / NFFT)
    table = np.stack([np.cos(angles), -np.sin(angles)], axis=0) * math.sqrt(2.0 / BINS)
    table = table.reshape(2, 16, PARTS, NB, LAGS).transpose(2, 1, 0, 3, 4)
    return table.reshape(2 * BINS, LAGS).astype(np.float32).astype(jnp.bfloat16)


def nt_dot(a, b):
    return lax.dot_general(a, b, (((1,), (1,)), ((), ())), preferred_element_type=F32)


def tn_dot(a, b):
    return lax.dot_general(a, b, (((0,), (0,)), ((), ())), preferred_element_type=F32)


def spectra_kernel(rec, table, mask, out, planes, rows, spec, power):
    for c in range(0, CH, 4):
        signal = rec[c : c + 4].astype(F32).reshape(4 * WIN, SEG)
        centred = signal - jnp.mean(signal, axis=-1, keepdims=True)
        spread = jnp.sqrt(jnp.mean(centred * centred, axis=-1, keepdims=True) + 1e-06)
        normal = centred / spread
        for t in range(SEG // 128):
            planes[t, c * WIN : (c + 4) * WIN, :] = normal[:, t * 128 : (t + 1) * 128]
    for w in range(WIN):
        for t in range(SEG // 128):
            rows[w * CH : (w + 1) * CH, t * 128 : (t + 1) * 128] = planes[
                t, pl.ds(w, CH, stride=WIN), :
            ].astype(BF)

    def multiply(i, carry):
        at = pl.ds(pl.multiple_of(i * 256, 256), 256)
        spec[at, :] = nt_dot(table[at, :], rows[...])
        return carry

    lax.fori_loop(0, 4, multiply, 0)
    power[0:8, :] = jnp.zeros((8, 512), F32)
    power[8 + BINS : 16 + BINS, :] = jnp.zeros((8, 512), F32)
    for k in range(0, BINS, 64):
        real, imag = spec[k : k + 64, :], spec[BINS + k : BINS + k + 64, :]
        power[8 + k : 72 + k, :] = real * real + imag * imag
    window = lax.broadcasted_iota(jnp.int32, (WIN, 512), 0)
    pick = (lax.broadcasted_iota(jnp.int32, (WIN, 512), 1) // CH == window).astype(BF)
    spread = jnp.dot(mask[...].astype(F32).astype(BF), pick, preferred_element_type=F32)
    channel = lax.broadcasted_iota(jnp.int32, (CH, 512), 0)
    own_lane = lax.broadcasted_iota(jnp.int32, (CH, 512), 1) % CH == channel
    valid = jnp.sum(jnp.where(own_lane, spread, 0.0), axis=0, keepdims=True)
    sent_mask = jnp.concatenate(
        [valid[:, i * 128 : (i + 1) * 128] for i in range(4)] + [jnp.zeros((4, 128), F32)], axis=0
    ).astype(BF)
    step = NB * PARTS
    for dst in range(16):
        k = dst * step
        total = power[4 + k : 4 + k + step, :]
        for offset in range(1, 2 * SMOOTH + 1):
            total = total + power[4 + k + offset : 4 + k + offset + step, :]
        bins = k + lax.broadcasted_iota(jnp.int32, (step, 512), 0)
        count = jnp.minimum(bins, SMOOTH) + jnp.minimum(BINS - 1 - bins, SMOOTH) + 1
        factor = valid / jnp.sqrt(total / count.astype(F32) + 0.1)
        for ri in range(2):
            white = (spec[ri * BINS + k : ri * BINS + k + step, :] * factor).astype(BF)
            for part in range(PARTS):
                for high in range(4):
                    at = part * PART_ROWS + (high * 2 + ri) * NB
                    out[dst, at : at + NB, :] = white[
                        part * NB : (part + 1) * NB, high * 128 : (high + 1) * 128
                    ]
        out[dst, MASK_ROW:SENT_ROWS, :] = sent_mask


def spectra(records, gap_mask):
    full = pl.BlockSpec(memory_space=pltpu.VMEM)
    return pl.pallas_call(
        spectra_kernel,
        out_shape=jax.ShapeDtypeStruct((16, SENT_ROWS, 128), BF),
        in_specs=[full] * 3,
        out_specs=full,
        scratch_shapes=[
            pltpu.VMEM((SEG // 128, 512, 128), F32),
            pltpu.VMEM((512, SEG), BF),
            pltpu.VMEM((2 * BINS, 512), F32),
            pltpu.VMEM((BINS + 16, 512), F32),
        ],
        compiler_params=pltpu.CompilerParams(vmem_limit_bytes=48 << 20),
        cost_estimate=pl.CostEstimate(flops=2 * 512 * SEG * 2 * BINS, bytes_accessed=8 << 20, transcendentals=0),
        name="spectra",
    )(records, jnp.asarray(forward_table()), gap_mask)


def blocks_to_lanes(parts):
    lane = lax.broadcasted_iota(jnp.int32, parts[0].shape, 1)
    low, odd = lane < 64, (lane // 32) % 2 == 0
    half = []
    a0, a1, a2, a3 = parts
    half = [
        jnp.where(low, a0, pltpu.roll(a2, 64, 1)),
        jnp.where(low, a1, pltpu.roll(a3, 64, 1)),
        jnp.where(low, pltpu.roll(a0, 64, 1), a2),
        jnp.where(low, pltpu.roll(a1, 64, 1), a3),
    ]
    return [
        jnp.where(odd, half[0], pltpu.roll(half[1], 32, 1)),
        jnp.where(odd, pltpu.roll(half[0], 96, 1), half[1]),
        jnp.where(odd, half[2], pltpu.roll(half[3], 32, 1)),
        jnp.where(odd, pltpu.roll(half[2], 96, 1), half[3]),
    ]


def cross_kernel(part, own, prev, out, planes, pairs):
    for block in range(7):
        for v in range(4):
            for ri in range(2):
                source, first = (
                    (prev.at[block * 4 + v], 0)
                    if block < 3
                    else (own.at[(block - 3) * 4 + v], part * PART_ROWS)
                )
                for high in range(4):
                    row = ((block * 2 + ri) * 4 + v) * 4 + high
                    at = first + (high * 2 + ri) * NB
                    planes[row * NB : (row + 1) * NB, :] = source[at : at + NB, :].astype(F32)
    lane = lax.broadcasted_iota(jnp.int32, (32, 128), 1)

    def one_bin(k, carry):
        def side(blocks):
            found = []
            for ri in range(2):
                parts = [
                    planes[pl.ds((block * 2 + ri) * 16 * NB + k, 16, stride=NB), :] for block in blocks
                ]
                found.append(jnp.concatenate(blocks_to_lanes(parts), axis=0))
            return found

        prev_real, prev_imag = side((0, 0, 1, 2))
        own_real, own_imag = side((3, 4, 5, 6))
        left = jnp.concatenate(
            [
                jnp.concatenate([own_real, own_imag], axis=0),
                jnp.concatenate([own_imag, -own_real], axis=0),
            ],
            axis=1,
        ).astype(BF)
        right = jnp.concatenate(
            [
                jnp.concatenate([prev_real, prev_imag], axis=0),
                jnp.concatenate([own_real, own_imag], axis=0),
            ],
            axis=1,
        ).astype(BF)
        product = tn_dot(left, right)
        for ri in range(2):
            for b in range(4):
                at = ri * 128 + b * 32
                first, second = product[at : at + 32, :128], product[at : at + 32, 128:]
                if b == 3:
                    value = second
                else:
                    value = pltpu.roll(first, 96 - 32 * b, 1)
                    if b:
                        value = jnp.where(lane < 96 - 32 * b, value, pltpu.roll(second, 96 - 32 * b, 1))
                pairs[pl.ds(at * NB + k, 32, stride=NB), :] = value
        return carry

    lax.fori_loop(0, NB, one_bin, 0, unroll=4)
    lanes = lax.broadcasted_iota(jnp.int32, (NB, 128), 1)
    for ri in range(2):
        for b in range(4):
            for v in range(4):
                for high in range(2):
                    row = ri * 128 + b * 32 + v * 8 + high * 4
                    p0, p1, p2, p3 = [pairs[(row + i) * NB : (row + i + 1) * NB, :] for i in range(4)]
                    p1, p2, p3 = pltpu.roll(p1, 96, 1), pltpu.roll(p2, 64, 1), pltpu.roll(p3, 32, 1)
                    target = out.at[b * 4 + v, ri, high]
                    target[:, 0:128] = jnp.where(lanes < 96, p0, p1).astype(BF)
                    target[:, 128:256] = jnp.where(lanes < 64, p1, p2).astype(BF)
                    target[:, 256:384] = jnp.where(lanes < 32, p2, p3).astype(BF)


def cross(part, own, prev):
    full = pl.BlockSpec(memory_space=pltpu.VMEM)
    return pl.pallas_call(
        functools.partial(cross_kernel, part),
        out_shape=jax.ShapeDtypeStruct((16, 2, 2, NB, 384), BF),
        in_specs=[full] * 2,
        out_specs=full,
        scratch_shapes=[
            pltpu.VMEM((7 * 32 * NB, 128), F32),
            pltpu.VMEM((256 * NB, 128), F32),
        ],
        compiler_params=pltpu.CompilerParams(vmem_limit_bytes=48 << 20),
        cost_estimate=pl.CostEstimate(flops=(8 << 30) // PARTS, bytes_accessed=(4 << 20) // PARTS, transcendentals=0),
        name="cross",
    )(own, prev)


def lag_kernel(*refs):
    crosses, (table, own_mask, partner_mask, out) = refs[:PARTS], refs[PARTS:]
    count = nt_dot(partner_mask[...], own_mask[...])
    scale = 1.0 / jnp.sqrt(jnp.maximum(count, 1.0))
    for high in range(2):
        left = jnp.concatenate(
            [value[:, :, high].reshape(2 * BINS // PARTS, 384) for value in crosses], axis=0
        )
        turned = left.T
        for at in range(0, LAGS, 512):
            end = min(at + 512, LAGS)
            lagged = jnp.dot(turned, table[:, at:end], preferred_element_type=F32)
            for low in range(4):
                c = high * 4 + low
                for s in range(3):
                    row = low * 96 + s * 32
                    out[2 - s, c, :, at:end] = (
                        lagged[row : row + 32] * scale[s * 32 : s * 32 + 32, c : c + 1]
                    ).astype(BF)


def lag_sums(crosses, own_mask, partner_mask):
    full = pl.BlockSpec(memory_space=pltpu.VMEM)
    return pl.pallas_call(
        lag_kernel,
        out_shape=jax.ShapeDtypeStruct((3, 8, CH, LAGS), BF),
        in_specs=[full] * (PARTS + 3),
        out_specs=full,
        compiler_params=pltpu.CompilerParams(vmem_limit_bytes=48 << 20),
        cost_estimate=pl.CostEstimate(flops=2 * 768 * 2 * BINS * LAGS, bytes_accessed=9 << 20, transcendentals=0),
        name="lag_sums",
    )(*crosses, jnp.asarray(inverse_table()), own_mask, partner_mask)


def shifted(value, axes, count, steps):
    return lax.ppermute(value, axes, [(i, (i + steps) % count) for i in range(count)])


def from_previous_group(value):
    return shifted(value, ("y", "zh"), 16, 1)


def per_device(records, gap_mask):
    own = lax.all_to_all(spectra(records, gap_mask), GROUP, 0, 0, tiled=True)
    edges = [p * PART_ROWS for p in range(PARTS)] + [SENT_ROWS]
    prevs = [from_previous_group(own[4:, edges[p] : edges[p + 1]]) for p in range(PARTS)]
    crosses = [
        lax.all_to_all(cross(p, own, prevs[p]), GROUP, 0, 0, tiled=True) for p in range(PARTS)
    ]
    masks = jnp.concatenate([prevs[-1][:, PART_ROWS : PART_ROWS + 4], own[:, MASK_ROW : MASK_ROW + 4]], axis=0)
    masks = lax.dynamic_slice_in_dim(masks, lax.axis_index("x") * 4, 16, 0)
    masks = masks.reshape(4, 16, 4, CH).transpose(0, 3, 1, 2).reshape(4 * CH, 64)
    own_mask = lax.dynamic_slice_in_dim(masks, 3 * CH + lax.axis_index(("zl", "core")) * 8, 8, 0)
    return lag_sums(crosses, own_mask, masks[: 3 * CH])


def solution(mesh):
    fine = Mesh(mesh.devices.reshape(4, 4, 4, 2, 2), ("y", "zh", "x", "zl", "core"))
    in_specs = (P(("y", "zh", "x"), ("zl", "core"), None), P(("y", "zh", "x"), ("zl", "core")))
    out_specs = P(None, ("y", "zh", "x", "zl", "core"), None, None)
    return jax.shard_map(
        per_device, mesh=fine, in_specs=in_specs, out_specs=out_specs, check_vma=False
    )
```

```python
import functools
import math

import jax
import jax.numpy as jnp
import numpy as np
from jax import lax
from jax.experimental import pallas as pl
from jax.experimental.pallas import tpu as pltpu
from jax.sharding import Mesh, PartitionSpec as P

SEG = 2048
NFFT = 4096
BINS = 512
SMOOTH = 4
LAGHALF = 1000
LAGS = 2001
CH = 32
WIN = 16
BF = jnp.bfloat16
F32 = jnp.float32
PARTS = 2
PART_BINS = BINS // PARTS
NB = PART_BINS // 16
PART_ROWS = 8 * NB
STRIDE = NB + 1
LAG_TILE = 1024
LAG_TILES = -(-LAGS // LAG_TILE)
MASK_ROW = PARTS * PART_ROWS
SENT_ROWS = MASK_ROW + 8
OWN_ROWS = SENT_ROWS
NEAR = 16
WIDE = PART_BINS + NEAR
CROSS_FLOPS = (0, 100 << 30)
GROUP = ("x", "zl", "core")
STATIONS = ("y", "zh", "x")


def forward_table(part):
    first = part * (PART_BINS - NEAR)
    phases = np.arange(first + 1, first + WIDE + 1)[:, None] * np.arange(SEG)[None, :] % NFFT
    angles = phases * (2.0 * math.pi / NFFT)
    table = np.concatenate([np.cos(angles), -np.sin(angles)], axis=0) / math.sqrt(SEG)
    return table.astype(np.float32).astype(jnp.bfloat16)


def inverse_table():
    phases = np.arange(1, BINS + 1)[:, None] * (np.arange(LAGS) - LAGHALF)[None, :] % NFFT
    angles = phases * (2.0 * math.pi / NFFT)
    table = np.stack([np.cos(angles), -np.sin(angles)], axis=0) * math.sqrt(2.0 / BINS)
    table = table.reshape(2, PARTS, 16, NB, LAGS).transpose(1, 2, 0, 3, 4)
    table = table.reshape(2 * BINS, LAGS).astype(np.float32).astype(jnp.bfloat16)
    table = np.pad(table, ((0, 0), (0, LAG_TILES * LAG_TILE - LAGS)))
    return table.reshape(2 * BINS, LAG_TILES, LAG_TILE).transpose(1, 0, 2)


def nt_dot(a, b):
    return lax.dot_general(a, b, (((1,), (1,)), ((), ())), preferred_element_type=F32)


def tn_dot(a, b):
    return lax.dot_general(a, b, (((0,), (0,)), ((), ())), preferred_element_type=F32)


def mask_lanes(mask):
    channel = lax.broadcasted_iota(jnp.int32, (CH, 512), 0)
    pick = (lax.broadcasted_iota(jnp.int32, (CH, 512), 1) % CH == channel).astype(BF)
    spread = jnp.dot(mask.astype(F32).astype(BF), pick, preferred_element_type=F32)
    window = lax.broadcasted_iota(jnp.int32, (WIN, 512), 0)
    own_lane = lax.broadcasted_iota(jnp.int32, (WIN, 512), 1) // CH == window
    valid = jnp.sum(jnp.where(own_lane, spread, 0.0), axis=0, keepdims=True)
    return [valid[:, i * 128 : (i + 1) * 128] for i in range(4)]


def whiten(part, rows, table, valid, out, spec, power):
    for ri in range(2):
        value = nt_dot(table[ri * WIDE : (ri + 1) * WIDE, :], rows[...])
        for high in range(4):
            spec[ri, high] = value[:, high * 128 : (high + 1) * 128]
    for high in range(4):
        power[high, 0:8, :] = jnp.zeros((8, 128), F32)
        power[high, 8 + WIDE : 16 + WIDE, :] = jnp.zeros((8, 128), F32)
        real, imag = spec[0, high], spec[1, high]
        power[high, 8 : 8 + WIDE, :] = real * real + imag * imag
    for dst in range(16):
        at = part * NEAR + dst * NB
        bins = part * PART_BINS + dst * NB + lax.broadcasted_iota(jnp.int32, (NB, 128), 0)
        count = jnp.minimum(bins, SMOOTH) + jnp.minimum(BINS - 1 - bins, SMOOTH) + 1
        inverse_count = 1.0 / count.astype(F32)
        for high in range(4):
            total = power[high, 4 + at : 4 + at + NB, :]
            for offset in range(5, 4 + 2 * SMOOTH + 1):
                total = total + power[high, at + offset : at + offset + NB, :]
            factor = valid[high] * lax.rsqrt(total * inverse_count + 0.1)
            for ri in range(2):
                row = part * PART_ROWS + (high * 2 + ri) * NB
                out[dst, row : row + NB, :] = (spec[ri, high, at : at + NB, :] * factor).astype(BF)


def spectra_kernel(rec_far, table_far, mask_far, out, mask, rec, rows, table, planes, spec, power, sems):
    chunk = 4
    copies = [
        pltpu.make_async_copy(rec_far.at[c : c + chunk], rec.at[c : c + chunk], sems.at[c // chunk])
        for c in range(0, CH, chunk)
    ]
    mask_copy = pltpu.make_async_copy(mask_far, mask, sems.at[CH // chunk + PARTS])
    for copy in copies + [mask_copy]:
        copy.start()
    table_copies = [
        pltpu.make_async_copy(table_far.at[part], table.at[part], sems.at[CH // chunk + part])
        for part in range(PARTS)
    ]
    for copy in table_copies:
        copy.start()
    for c in range(0, CH, chunk):
        copies[c // chunk].wait()
        signal = rec[c : c + chunk].astype(F32).reshape(chunk * WIN, SEG)
        centred = signal - jnp.mean(signal, axis=-1, keepdims=True)
        spread = jnp.sqrt(jnp.mean(centred * centred, axis=-1, keepdims=True) + 1e-06)
        normal = centred * (1.0 / spread)
        for t in range(SEG // 128):
            for i in range(chunk):
                planes[t, (c + i) * STRIDE : (c + i) * STRIDE + WIN, :] = normal[i * WIN : (i + 1) * WIN, t * 128 : (t + 1) * 128]
    for w in range(WIN):
        for t in range(SEG // 128):
            rows[w * CH : (w + 1) * CH, t * 128 : (t + 1) * 128] = planes[
                t, pl.ds(w, CH, stride=STRIDE), :
            ].astype(BF)
    mask_copy.wait()
    valid = mask_lanes(mask[...])
    sent_mask = jnp.concatenate(valid + [jnp.zeros((4, 128), F32)], axis=0).astype(BF)
    for dst in range(16):
        out[dst, MASK_ROW:SENT_ROWS, :] = sent_mask
    for part in range(PARTS):
        table_copies[part].wait()
        whiten(part, rows, table.at[part], valid, out, spec, power)


def spectra(records, gap_mask):
    near, far = pl.BlockSpec(memory_space=pltpu.VMEM), pl.BlockSpec(memory_space=pltpu.HBM)
    return pl.pallas_call(
        spectra_kernel,
        out_shape=jax.ShapeDtypeStruct((16, SENT_ROWS, 128), BF),
        in_specs=[far] * 3,
        out_specs=near,
        scratch_shapes=[
            pltpu.VMEM((WIN, CH), jnp.int32),
            pltpu.VMEM((CH, WIN, SEG), BF),
            pltpu.VMEM((512, SEG), BF),
            pltpu.VMEM((PARTS, 2 * WIDE, SEG), BF),
            pltpu.VMEM((SEG // 128, CH * STRIDE, 128), F32),
            pltpu.VMEM((2, 4, WIDE, 128), F32),
            pltpu.VMEM((4, WIDE + 16, 128), F32),
            pltpu.SemaphoreType.DMA((9 + PARTS,)),
        ],
        compiler_params=pltpu.CompilerParams(vmem_limit_bytes=62 << 20),
        cost_estimate=pl.CostEstimate(
            flops=2 * 512 * SEG * 2 * BINS, bytes_accessed=8 << 20, transcendentals=0
        ),
        name="spectra",
    )(records, jnp.asarray(np.stack([forward_table(p) for p in range(PARTS)])), gap_mask.T)


def blocks_to_lanes(parts):
    lane = lax.broadcasted_iota(jnp.int32, parts[0].shape, 1)
    low, odd = lane < 64, (lane // 32) % 2 == 0
    half = []
    a0, a1, a2, a3 = parts
    half = [
        jnp.where(low, a0, pltpu.roll(a2, 64, 1)),
        jnp.where(low, a1, pltpu.roll(a3, 64, 1)),
        jnp.where(low, pltpu.roll(a0, 64, 1), a2),
        jnp.where(low, pltpu.roll(a1, 64, 1), a3),
    ]
    return [
        jnp.where(odd, half[0], pltpu.roll(half[1], 32, 1)),
        jnp.where(odd, pltpu.roll(half[0], 96, 1), half[1]),
        jnp.where(odd, half[2], pltpu.roll(half[3], 32, 1)),
        jnp.where(odd, pltpu.roll(half[2], 96, 1), half[3]),
    ]


def cross_kernel(part, own, prev, out, planes, pairs):
    for block in range(7):
        for v in range(4):
            for ri in range(2):
                source, first = (
                    (prev.at[block * 4 + v], 0)
                    if block < 3
                    else (own.at[(block - 3) * 4 + v], part * PART_ROWS)
                )
                for high in range(4):
                    row = ((block * 2 + ri) * 4 + v) * 4 + high
                    at = first + (high * 2 + ri) * NB
                    planes[row * STRIDE : row * STRIDE + NB, :] = source[at : at + NB, :].astype(F32)
    lane = lax.broadcasted_iota(jnp.int32, (32, 128), 1)

    def one_bin(k, carry):
        def side(blocks):
            found = []
            for ri in range(2):
                parts = [
                    planes[pl.ds((block * 2 + ri) * 16 * STRIDE + k, 16, stride=STRIDE), :] for block in blocks
                ]
                found.append(jnp.concatenate(blocks_to_lanes(parts), axis=0))
            return found

        prev_real, prev_imag = side((0, 0, 1, 2))
        own_real, own_imag = side((3, 4, 5, 6))
        left = jnp.concatenate(
            [
                jnp.concatenate([own_real, own_imag], axis=0),
                jnp.concatenate([own_imag, -own_real], axis=0),
            ],
            axis=1,
        ).astype(BF)
        right = jnp.concatenate(
            [
                jnp.concatenate([prev_real, prev_imag], axis=0),
                jnp.concatenate([own_real, own_imag], axis=0),
            ],
            axis=1,
        ).astype(BF)
        product = tn_dot(left, right)
        for ri in range(2):
            for b in range(4):
                at = ri * 128 + b * 32
                first, second = product[at : at + 32, :128], product[at : at + 32, 128:]
                if b == 3:
                    value = second
                else:
                    value = pltpu.roll(first, 96 - 32 * b, 1)
                    if b:
                        value = jnp.where(lane < 96 - 32 * b, value, pltpu.roll(second, 96 - 32 * b, 1))
                pairs[pl.ds(at * STRIDE + k, 32, stride=STRIDE), :] = value
        return carry

    lax.fori_loop(0, NB, one_bin, 0, unroll=4)
    lanes = lax.broadcasted_iota(jnp.int32, (NB, 128), 1)
    for ri in range(2):
        for b in range(4):
            for v in range(4):
                for high in range(2):
                    row = ri * 128 + b * 32 + v * 8 + high * 4
                    p0, p1, p2, p3 = [pairs[(row + i) * STRIDE : (row + i) * STRIDE + NB, :] for i in range(4)]
                    p1, p2, p3 = pltpu.roll(p1, 96, 1), pltpu.roll(p2, 64, 1), pltpu.roll(p3, 32, 1)
                    target = out.at[b * 4 + v, ri, high]
                    target[:, 0:128] = jnp.where(lanes < 96, p0, p1).astype(BF)
                    target[:, 128:256] = jnp.where(lanes < 64, p1, p2).astype(BF)
                    target[:, 256:384] = jnp.where(lanes < 32, p2, p3).astype(BF)


def cross(part, own, prev):
    full = pl.BlockSpec(memory_space=pltpu.VMEM)
    return pl.pallas_call(
        functools.partial(cross_kernel, part),
        out_shape=jax.ShapeDtypeStruct((16, 2, 2, NB, 384), BF),
        in_specs=[full] * 2,
        out_specs=full,
        scratch_shapes=[
            pltpu.VMEM((7 * 32 * STRIDE, 128), F32),
            pltpu.VMEM((256 * STRIDE, 128), F32),
        ],
        compiler_params=pltpu.CompilerParams(vmem_limit_bytes=48 << 20),
        cost_estimate=pl.CostEstimate(flops=CROSS_FLOPS[part], bytes_accessed=1 << 20, transcendentals=0),
        name="cross",
    )(own, prev)


def turn_kernel(value, out):
    for high in range(2):
        out[high * 384 : (high + 1) * 384, :] = value[:, :, high].reshape(2 * PART_BINS, 384).T


def turn(value):
    near = pl.BlockSpec(memory_space=pltpu.VMEM)
    return pl.pallas_call(
        turn_kernel,
        out_shape=jax.ShapeDtypeStruct((768, 2 * PART_BINS), BF),
        in_specs=[near],
        out_specs=near,
        compiler_params=pltpu.CompilerParams(vmem_limit_bytes=8 << 20),
        cost_estimate=pl.CostEstimate(flops=0, bytes_accessed=4 << 20, transcendentals=0),
        name="turn",
    )(value)


def lag_kernel(first, second, table, own_mask, partner_mask, out, turned, scales):
    @pl.when(pl.program_id(0) == 0)
    def _():
        turned[:, : 2 * PART_BINS] = first[...]
        for high in range(2):
            turned[high * 384 : (high + 1) * 384, 2 * PART_BINS :] = (
                second[:, :, high].reshape(2 * PART_BINS, 384).T
            )
        count = nt_dot(partner_mask[...], own_mask[...])
        scale = 1.0 / jnp.sqrt(jnp.maximum(count, 1.0))
        for c in range(8):
            scales[c * 96 : (c + 1) * 96, :] = jnp.broadcast_to(scale[:, c : c + 1], (96, 128))

    lagged = jnp.dot(turned[...], table[0], preferred_element_type=F32)
    for c in range(8):
        for s in range(3):
            row = c * 96 + s * 32
            for at in range(0, LAG_TILE, 128):
                out[2 - s, c, :, at : at + 128] = (
                    lagged[row : row + 32, at : at + 128] * scales[row : row + 32, :]
                ).astype(BF)


def lag_sums(first, second, own_mask, partner_mask):
    return pl.pallas_call(
        lag_kernel,
        grid=(LAG_TILES,),
        out_shape=jax.ShapeDtypeStruct((3, 8, CH, LAGS), BF),
        in_specs=[
            pl.BlockSpec((768, 2 * PART_BINS), lambda i: (0, 0)),
            pl.BlockSpec((16, 2, 2, NB, 384), lambda i: (0, 0, 0, 0, 0)),
            pl.BlockSpec((1, 2 * BINS, LAG_TILE), lambda i: (i, 0, 0)),
            pl.BlockSpec((8, 64), lambda i: (0, 0)),
            pl.BlockSpec((3 * CH, 64), lambda i: (0, 0)),
        ],
        out_specs=pl.BlockSpec((3, 8, CH, LAG_TILE), lambda i: (0, 0, 0, i)),
        scratch_shapes=[pltpu.VMEM((768, 2 * BINS), BF), pltpu.VMEM((768, 128), F32)],
        compiler_params=pltpu.CompilerParams(vmem_limit_bytes=62 << 20),
        cost_estimate=pl.CostEstimate(
            flops=2 * 768 * 2 * BINS * LAGS, bytes_accessed=9 << 20, transcendentals=0
        ),
        name="lag_sums",
    )(first, second, jnp.asarray(inverse_table()), own_mask, partner_mask)


def shifted(value, axes, count, steps):
    return lax.ppermute(value, axes, [(i, (i + steps) % count) for i in range(count)])


def from_previous_group(value):
    return shifted(value, ("y", "zh"), 16, 1)


def per_device(records, gap_mask):
    own = lax.all_to_all(spectra(records, gap_mask), GROUP, 0, 0, tiled=True)
    prevs = [from_previous_group(own[4:, :PART_ROWS])]
    halo, prevs[0] = lax.optimization_barrier((own[4:, PART_ROWS:], prevs[0]))
    prevs.append(from_previous_group(halo))
    crosses = [
        lax.all_to_all(cross(p, own, prevs[p]), GROUP, 0, 0, tiled=True) for p in range(PARTS)
    ]
    masks = jnp.concatenate([prevs[-1][:, PART_ROWS : PART_ROWS + 4], own[:, MASK_ROW : MASK_ROW + 4]], axis=0)
    masks = lax.dynamic_slice_in_dim(masks, lax.axis_index("x") * 4, 16, 0)
    masks = masks.reshape(4, 16, 4, CH).transpose(0, 3, 1, 2).reshape(4 * CH, 64)
    own_mask = lax.dynamic_slice_in_dim(masks, 3 * CH + lax.axis_index(("zl", "core")) * 8, 8, 0)
    return lag_sums(turn(crosses[0]), crosses[1], own_mask, masks[: 3 * CH])


def solution(mesh):
    fine = Mesh(mesh.devices.reshape(4, 4, 4, 2, 2), ("y", "zh", "x", "zl", "core"))
    in_specs = (P(("y", "zh", "x"), ("zl", "core"), None), P(("y", "zh", "x"), ("zl", "core")))
    out_specs = P(None, ("y", "zh", "x", "zl", "core"), None, None)
    return jax.shard_map(
        per_device, mesh=fine, in_specs=in_specs, out_specs=out_specs, check_vma=False
    )
```

```python
import functools
import math

import jax
import jax.numpy as jnp
import numpy as np
from jax import lax
from jax.experimental import pallas as pl
from jax.experimental.pallas import tpu as pltpu
from jax.sharding import Mesh, PartitionSpec as P

SEG = 2048
NFFT = 4096
BINS = 512
SMOOTH = 4
LAGHALF = 1000
LAGS = 2001
CH = 32
WIN = 16
BF = jnp.bfloat16
F32 = jnp.float32
PARTS = 2
PART_BINS = BINS // PARTS
NB = PART_BINS // 16
PART_ROWS = 8 * NB
STRIDE = NB + 1
MASK_ROW = PARTS * PART_ROWS
SENT_ROWS = MASK_ROW + 8
OWN_ROWS = SENT_ROWS
NEAR = 16
WIDE = PART_BINS + NEAR
CROSS_FLOPS = (0, 100 << 30)
GROUP = ("x", "zl", "core")
STATIONS = ("y", "zh", "x")


def forward_table(part):
    first = part * (PART_BINS - NEAR)
    phases = np.arange(first + 1, first + WIDE + 1)[:, None] * np.arange(SEG)[None, :] % NFFT
    angles = phases * (2.0 * math.pi / NFFT)
    table = np.concatenate([np.cos(angles), -np.sin(angles)], axis=0) / math.sqrt(SEG)
    return table.astype(np.float32).astype(jnp.bfloat16)


def inverse_table():
    phases = np.arange(1, BINS + 1)[:, None] * np.arange(LAGHALF, -1, -1)[None, :] % NFFT
    angles = phases * (2.0 * math.pi / NFFT)
    table = np.stack([np.cos(angles), -np.sin(angles)], axis=0) * math.sqrt(2.0 / BINS)
    return np.pad(table, ((0, 0), (0, 0), (0, 23))).astype(np.float32).astype(jnp.bfloat16)


def nt_dot(a, b):
    return lax.dot_general(a, b, (((1,), (1,)), ((), ())), preferred_element_type=F32)


def tn_dot(a, b):
    return lax.dot_general(a, b, (((0,), (0,)), ((), ())), preferred_element_type=F32)


def mask_lanes(mask):
    channel = lax.broadcasted_iota(jnp.int32, (CH, 512), 0)
    pick = (lax.broadcasted_iota(jnp.int32, (CH, 512), 1) % CH == channel).astype(BF)
    spread = jnp.dot(mask.astype(F32).astype(BF), pick, preferred_element_type=F32)
    window = lax.broadcasted_iota(jnp.int32, (WIN, 512), 0)
    own_lane = lax.broadcasted_iota(jnp.int32, (WIN, 512), 1) // CH == window
    valid = jnp.sum(jnp.where(own_lane, spread, 0.0), axis=0, keepdims=True)
    return [valid[:, i * 128 : (i + 1) * 128] for i in range(4)]


def whiten(part, rows, table, valid, out, spec, power):
    for ri in range(2):
        value = nt_dot(table[ri * WIDE : (ri + 1) * WIDE, :], rows[...])
        for high in range(4):
            spec[ri, high] = value[:, high * 128 : (high + 1) * 128]
    for high in range(4):
        power[high, 0:8, :] = jnp.zeros((8, 128), F32)
        power[high, 8 + WIDE : 16 + WIDE, :] = jnp.zeros((8, 128), F32)
        real, imag = spec[0, high], spec[1, high]
        power[high, 8 : 8 + WIDE, :] = real * real + imag * imag
    for dst in range(16):
        at = part * NEAR + dst * NB
        bins = part * PART_BINS + dst * NB + lax.broadcasted_iota(jnp.int32, (NB, 128), 0)
        count = jnp.minimum(bins, SMOOTH) + jnp.minimum(BINS - 1 - bins, SMOOTH) + 1
        inverse_count = 1.0 / count.astype(F32)
        for high in range(4):
            total = power[high, 4 + at : 4 + at + NB, :]
            for offset in range(5, 4 + 2 * SMOOTH + 1):
                total = total + power[high, at + offset : at + offset + NB, :]
            factor = valid[high] * lax.rsqrt(total * inverse_count + 0.1)
            for ri in range(2):
                row = part * PART_ROWS + (high * 2 + ri) * NB
                out[dst, row : row + NB, :] = (spec[ri, high, at : at + NB, :] * factor).astype(BF)


def spectra_kernel(rec_far, table_far, mask_far, out, mask, rec, rows, table, planes, spec, power, sems):
    chunk = 4
    copies = [
        pltpu.make_async_copy(rec_far.at[c : c + chunk], rec.at[c : c + chunk], sems.at[c // chunk])
        for c in range(0, CH, chunk)
    ]
    mask_copy = pltpu.make_async_copy(mask_far, mask, sems.at[CH // chunk + PARTS])
    for copy in copies + [mask_copy]:
        copy.start()
    table_copies = [
        pltpu.make_async_copy(table_far.at[part], table.at[part], sems.at[CH // chunk + part])
        for part in range(PARTS)
    ]
    for copy in table_copies:
        copy.start()
    for c in range(0, CH, chunk):
        copies[c // chunk].wait()
        signal = rec[c : c + chunk].astype(F32).reshape(chunk * WIN, SEG)
        centred = signal - jnp.mean(signal, axis=-1, keepdims=True)
        spread = jnp.sqrt(jnp.mean(centred * centred, axis=-1, keepdims=True) + 1e-06)
        normal = centred * (1.0 / spread)
        for t in range(SEG // 128):
            for i in range(chunk):
                planes[t, (c + i) * STRIDE : (c + i) * STRIDE + WIN, :] = normal[i * WIN : (i + 1) * WIN, t * 128 : (t + 1) * 128]
    for w in range(WIN):
        for t in range(SEG // 128):
            rows[w * CH : (w + 1) * CH, t * 128 : (t + 1) * 128] = planes[
                t, pl.ds(w, CH, stride=STRIDE), :
            ].astype(BF)
    mask_copy.wait()
    valid = mask_lanes(mask[...])
    sent_mask = jnp.concatenate(valid + [jnp.zeros((4, 128), F32)], axis=0).astype(BF)
    for dst in range(16):
        out[dst, MASK_ROW:SENT_ROWS, :] = sent_mask
    for part in range(PARTS):
        table_copies[part].wait()
        whiten(part, rows, table.at[part], valid, out, spec, power)


def spectra(records, gap_mask):
    near, far = pl.BlockSpec(memory_space=pltpu.VMEM), pl.BlockSpec(memory_space=pltpu.HBM)
    return pl.pallas_call(
        spectra_kernel,
        out_shape=jax.ShapeDtypeStruct((16, SENT_ROWS, 128), BF),
        in_specs=[far] * 3,
        out_specs=near,
        scratch_shapes=[
            pltpu.VMEM((WIN, CH), jnp.int32),
            pltpu.VMEM((CH, WIN, SEG), BF),
            pltpu.VMEM((512, SEG), BF),
            pltpu.VMEM((PARTS, 2 * WIDE, SEG), BF),
            pltpu.VMEM((SEG // 128, CH * STRIDE + 32, 128), F32),
            pltpu.VMEM((2, 4, WIDE, 128), F32),
            pltpu.VMEM((4, WIDE + 16, 128), F32),
            pltpu.SemaphoreType.DMA((9 + PARTS,)),
        ],
        compiler_params=pltpu.CompilerParams(vmem_limit_bytes=62 << 20),
        cost_estimate=pl.CostEstimate(
            flops=2 * 512 * SEG * 2 * BINS, bytes_accessed=8 << 20, transcendentals=0
        ),
        name="spectra",
    )(records, jnp.asarray(np.stack([forward_table(p) for p in range(PARTS)])), gap_mask.T)


def rolled(value, lanes):
    return pltpu.roll(value, lanes % 128, 1) if lanes % 128 else value


def blocks_to_lanes(parts):
    slot = lax.broadcasted_iota(jnp.int32, parts[0].shape, 1) // 32
    found = []
    for low in range(4):
        value = parts[-low % 4]
        for at in range(1, 4):
            value = jnp.where(slot == at, parts[(at - low) % 4], value)
        found.append(rolled(value, -32 * low))
    return found


def cross_kernel(part, own, prev, out_far, planes, pairs, out, sems):
    for block in range(7):
        for v in range(4):
            for ri in range(2):
                source, first = (
                    (prev.at[block * 4 + v], 0)
                    if block < 3
                    else (own.at[(block - 3) * 4 + v], part * PART_ROWS)
                )
                for high in range(4):
                    row = ((block * 2 + ri) * 4 + v) * 4 + high
                    at = first + (high * 2 + ri) * NB
                    value = source[at : at + NB, :].astype(F32)
                    planes[row * STRIDE : row * STRIDE + NB, :] = rolled(value, 32 * (block + 1 if block < 3 else block - 3))
    lane = lax.broadcasted_iota(jnp.int32, (32, 128), 1)

    def one_bin(k, carry):
        def side(blocks):
            found = []
            for ri in range(2):
                parts = [
                    planes[pl.ds((block * 2 + ri) * 16 * STRIDE + k, 16, stride=STRIDE), :] for block in blocks
                ]
                found.append(jnp.concatenate(blocks_to_lanes(parts), axis=0))
            return found

        prev_real, prev_imag = side((0, 0, 1, 2))
        own_real, own_imag = side((3, 4, 5, 6))
        left = jnp.concatenate(
            [
                jnp.concatenate([own_real, own_imag], axis=0),
                jnp.concatenate([own_imag, -own_real], axis=0),
            ],
            axis=1,
        ).astype(BF)
        right = jnp.concatenate(
            [
                jnp.concatenate([prev_real, prev_imag], axis=0),
                jnp.concatenate([own_real, own_imag], axis=0),
            ],
            axis=1,
        ).astype(BF)
        product = tn_dot(left, right)
        for ri in range(2):
            for b in range(4):
                at = ri * 128 + b * 32
                first, second = product[at : at + 32, :128], product[at : at + 32, 128:]
                value = jnp.where(lane < 32 * b + 32, second, first)
                pairs[pl.ds(at * STRIDE + k, 32, stride=STRIDE), :] = value
        return carry

    lax.fori_loop(0, NB, one_bin, 0, unroll=8)
    lanes = lax.broadcasted_iota(jnp.int32, (NB, 128), 1)
    copies = []
    for b in range(4):
        for ri in range(2):
            for v in range(4):
                for high in range(2):
                    row = ri * 128 + b * 32 + v * 8 + high * 4
                    p0, p1, p2, p3 = [pairs[(row + i) * STRIDE : (row + i) * STRIDE + NB, :] for i in range(4)]
                    first = 32 * b + 32
                    p0, p1 = rolled(p0, -first), rolled(p1, 96 - first)
                    p2, p3 = rolled(p2, 64 - first), rolled(p3, 32 - first)
                    target = out.at[b * 4 + v, ri, high]
                    target[:, 0:128] = jnp.where(lanes < 96, p0, p1).astype(BF)
                    target[:, 128:256] = jnp.where(lanes < 64, p1, p2).astype(BF)
                    target[:, 256:384] = jnp.where(lanes < 32, p2, p3).astype(BF)
        dsts = pl.ds(b * 4, 4)
        copies.append(pltpu.make_async_copy(out.at[dsts], out_far.at[dsts], sems.at[b]))
        copies[b].start()
    for copy in copies:
        copy.wait()


def cross(part, own, prev):
    full = pl.BlockSpec(memory_space=pltpu.VMEM)
    return pl.pallas_call(
        functools.partial(cross_kernel, part),
        out_shape=jax.ShapeDtypeStruct((16, 2, 2, NB, 384), BF),
        in_specs=[full] * 2,
        out_specs=pl.BlockSpec(memory_space=pltpu.HBM),
        scratch_shapes=[
            pltpu.VMEM((7 * 32 * STRIDE + 32, 128), F32),
            pltpu.VMEM((256 * STRIDE + 32, 128), F32),
            pltpu.VMEM((16, 2, 2, NB, 384), BF),
            pltpu.SemaphoreType.DMA((4,)),
        ],
        compiler_params=pltpu.CompilerParams(vmem_limit_bytes=48 << 20),
        cost_estimate=pl.CostEstimate(flops=CROSS_FLOPS[part], bytes_accessed=1 << 20, transcendentals=0),
        name="cross",
    )(own, prev)


def turned(value, ri, high):
    return value[:, ri, high].reshape(PART_BINS, 384).T


def turn_kernel(value, own_mask, partner_mask, table_far, out, scales, table, sem):
    copy = pltpu.make_async_copy(table_far, table, sem)
    copy.start()
    for ri in range(2):
        for high in range(2):
            out[ri, high * 384 : (high + 1) * 384, :] = turned(value, ri, high)
    count = nt_dot(partner_mask[...], own_mask[...])
    scale = 1.0 / jnp.sqrt(jnp.maximum(count, 1.0))
    for c in range(8):
        scales[c * 96 : (c + 1) * 96, :] = jnp.broadcast_to(scale[:, c : c + 1], (96, 128))
    copy.wait()


def turn(value, own_mask, partner_mask):
    near = pl.BlockSpec(memory_space=pltpu.VMEM)
    return pl.pallas_call(
        turn_kernel,
        out_shape=[
            jax.ShapeDtypeStruct((2, 768, PART_BINS), BF),
            jax.ShapeDtypeStruct((768, 128), F32),
            jax.ShapeDtypeStruct((BINS, 1024), BF),
        ],
        in_specs=[near] * 3 + [pl.BlockSpec(memory_space=pltpu.HBM)],
        out_specs=[near] * 3,
        scratch_shapes=[pltpu.SemaphoreType.DMA],
        compiler_params=pltpu.CompilerParams(vmem_limit_bytes=8 << 20),
        cost_estimate=pl.CostEstimate(flops=0, bytes_accessed=4 << 20, transcendentals=0),
        name="turn",
    )(value, own_mask, partner_mask, jnp.asarray(inverse_table()[0]))


def lag_kernel(first, second, scales, cosines, sines, out, left, back):
    for ri in range(2):
        left[ri, :, :PART_BINS] = first[ri]
        left[ri, :, PART_BINS:] = turned(second, ri, 0)
    row = lax.broadcasted_iota(jnp.int32, (256, 256), 0)
    col = lax.broadcasted_iota(jnp.int32, (256, 256), 1)
    reverse = ((row // 128 == col // 128) & ((row + col) % 128 == 80)).astype(BF)
    lane = lax.broadcasted_iota(jnp.int32, (CH, 128), 1)
    for at in (512, 0):
        even = jnp.dot(left[0], cosines[:, at : at + 512], preferred_element_type=F32)
        odd = jnp.dot(left[1], sines[:, at : at + 512], preferred_element_type=F32)
        ahead, behind = even + odd, even - odd
        for pair in range(2):
            both = []
            for tile in range(2):
                lanes = slice((pair * 2 + tile) * 128, (pair * 2 + tile + 1) * 128)
                both.append((ahead[:, lanes] * scales[...]).astype(BF))
            back[:, at + pair * 256 : at + pair * 256 + 256] = jnp.dot(
                jnp.concatenate(both, axis=1), reverse, preferred_element_type=F32
            )
        for low in range(4):
            for s in range(3):
                rows = slice(low * 96 + s * 32, low * 96 + s * 32 + 32)
                for tile in range(4):
                    lanes = slice(tile * 128, (tile + 1) * 128)
                    value = behind[rows, lanes] * scales[rows, :]
                    if at + tile * 128 == 896:
                        value = jnp.where(lane <= LAGHALF - 896, value, back[rows, 896:1024])
                    out[2 - s, low, :, at + tile * 128 : at + (tile + 1) * 128] = value.astype(BF)
    for low in range(4):
        for s in range(3):
            rows = slice(low * 96 + s * 32, low * 96 + s * 32 + 32)
            for tile in range(8):
                high_lanes = back[rows, (7 - tile) * 128 : (8 - tile) * 128]
                if tile < 7:
                    low_lanes = back[rows, (6 - tile) * 128 : (7 - tile) * 128]
                    value = jnp.where(lane <= 80, high_lanes, low_lanes)
                    out[2 - s, low, :, 1024 + tile * 128 : 1152 + tile * 128] = value.astype(BF)
                else:
                    out[2 - s, low, :, 1920:LAGS] = high_lanes[:, : LAGS - 1920].astype(BF)


def lag_sums(first, second, scales, cosines):
    return pl.pallas_call(
        lag_kernel,
        grid=(2,),
        out_shape=jax.ShapeDtypeStruct((3, 8, CH, LAGS), BF),
        in_specs=[
            pl.BlockSpec((2, 384, PART_BINS), lambda h: (0, h, 0)),
            pl.BlockSpec((16, 2, 1, NB, 384), lambda h: (0, 0, h, 0, 0)),
            pl.BlockSpec((384, 128), lambda h: (h, 0)),
            pl.BlockSpec((BINS, 1024), lambda h: (0, 0)),
            pl.BlockSpec((BINS, 1024), lambda h: (0, 0)),
        ],
        out_specs=pl.BlockSpec((3, 4, CH, LAGS), lambda h: (0, h, 0, 0)),
        scratch_shapes=[pltpu.VMEM((2, 384, BINS), BF), pltpu.VMEM((384, 1024), F32)],
        compiler_params=pltpu.CompilerParams(vmem_limit_bytes=59 << 20),
        cost_estimate=pl.CostEstimate(
            flops=768 * 2 * BINS * LAGS, bytes_accessed=7 << 20, transcendentals=0
        ),
        name="lag_sums",
    )(first, second, scales, cosines, jnp.asarray(inverse_table()[1]))


def shifted(value, axes, count, steps):
    return lax.ppermute(value, axes, [(i, (i + steps) % count) for i in range(count)])


def from_previous_group(value):
    return shifted(value, ("y", "zh"), 16, 1)


def per_device(records, gap_mask):
    own = lax.all_to_all(spectra(records, gap_mask), GROUP, 0, 0, tiled=True)
    prevs = [from_previous_group(own[4:, :PART_ROWS])]
    halo, prevs[0] = lax.optimization_barrier((own[4:, PART_ROWS:], prevs[0]))
    prevs.append(from_previous_group(halo))
    crosses = [
        lax.all_to_all(cross(p, own, prevs[p]), GROUP, 0, 0, tiled=True) for p in range(PARTS)
    ]
    masks = jnp.concatenate([prevs[-1][:, PART_ROWS : PART_ROWS + 4], own[:, MASK_ROW : MASK_ROW + 4]], axis=0)
    masks = lax.dynamic_slice_in_dim(masks, lax.axis_index("x") * 4, 16, 0)
    masks = masks.reshape(4, 16, 4, CH).transpose(0, 3, 1, 2).reshape(4 * CH, 64)
    own_mask = lax.dynamic_slice_in_dim(masks, 3 * CH + lax.axis_index(("zl", "core")) * 8, 8, 0)
    first, scales, cosines = turn(crosses[0], own_mask, masks[: 3 * CH])
    return lag_sums(first, crosses[1], scales, cosines)


def solution(mesh):
    fine = Mesh(mesh.devices.reshape(4, 4, 4, 2, 2), ("y", "zh", "x", "zl", "core"))
    in_specs = (P(("y", "zh", "x"), ("zl", "core"), None), P(("y", "zh", "x"), ("zl", "core")))
    out_specs = P(None, ("y", "zh", "x", "zl", "core"), None, None)
    return jax.shard_map(
        per_device, mesh=fine, in_specs=in_specs, out_specs=out_specs, check_vma=False
    )
```

```python
import functools
import math

import jax
import jax.numpy as jnp
import numpy as np
from jax import lax
from jax.experimental import pallas as pl
from jax.experimental.pallas import tpu as pltpu
from jax.sharding import Mesh, PartitionSpec as P

SEG = 2048
NFFT = 4096
BINS = 512
SMOOTH = 4
LAGHALF = 1000
LAGS = 2001
CH = 32
WIN = 16
BF = jnp.bfloat16
F32 = jnp.float32
PARTS = 2
PART_BINS = BINS // PARTS
NB = PART_BINS // 16
PART_ROWS = 8 * NB
STRIDE = NB + 1
MASK_ROW = PARTS * PART_ROWS
SENT_ROWS = MASK_ROW + 8
OWN_ROWS = SENT_ROWS
NEAR = 16
WIDE = PART_BINS + NEAR
CROSS_FLOPS = (0, 100 << 30)
GROUP = ("x", "zl", "core")
STATIONS = ("y", "zh", "x")


def forward_table(part):
    first = part * (PART_BINS - NEAR)
    phases = np.arange(first + 1, first + WIDE + 1)[:, None] * np.arange(SEG)[None, :] % NFFT
    angles = phases * (2.0 * math.pi / NFFT)
    table = np.concatenate([np.cos(angles), -np.sin(angles)], axis=0) / math.sqrt(SEG)
    return table.astype(np.float32).astype(jnp.bfloat16)


def inverse_table():
    phases = np.arange(1, BINS + 1)[:, None] * np.arange(LAGHALF, -1, -1)[None, :] % NFFT
    angles = phases * (2.0 * math.pi / NFFT)
    table = np.stack([np.cos(angles), -np.sin(angles)], axis=0) * math.sqrt(2.0 / BINS)
    return np.pad(table, ((0, 0), (0, 0), (0, 23))).astype(np.float32).astype(jnp.bfloat16)


def nt_dot(a, b):
    return lax.dot_general(a, b, (((1,), (1,)), ((), ())), preferred_element_type=F32)


def tn_dot(a, b):
    return lax.dot_general(a, b, (((0,), (0,)), ((), ())), preferred_element_type=F32)


def mask_lanes(mask):
    channel = lax.broadcasted_iota(jnp.int32, (CH, 512), 0)
    pick = (lax.broadcasted_iota(jnp.int32, (CH, 512), 1) % CH == channel).astype(BF)
    spread = jnp.dot(mask.astype(F32).astype(BF), pick, preferred_element_type=F32)
    window = lax.broadcasted_iota(jnp.int32, (WIN, 512), 0)
    own_lane = lax.broadcasted_iota(jnp.int32, (WIN, 512), 1) // CH == window
    valid = jnp.sum(jnp.where(own_lane, spread, 0.0), axis=0, keepdims=True)
    return [valid[:, i * 128 : (i + 1) * 128] for i in range(4)]


def multiply(rows, table, spec, power):
    for ri in range(2):
        value = nt_dot(table[ri * WIDE : (ri + 1) * WIDE, :], rows[...])
        for high in range(4):
            spec[ri, high] = value[:, high * 128 : (high + 1) * 128]
    for high in range(4):
        power[high, 0:8, :] = jnp.zeros((8, 128), F32)
        power[high, 8 + WIDE : 16 + WIDE, :] = jnp.zeros((8, 128), F32)
        real, imag = spec[0, high], spec[1, high]
        power[high, 8 : 8 + WIDE, :] = real * real + imag * imag


def whiten(part, dst, valid, out, spec, power):
    at = part * NEAR + dst * NB
    bins = part * PART_BINS + dst * NB + lax.broadcasted_iota(jnp.int32, (NB, 128), 0)
    count = jnp.minimum(bins, SMOOTH) + jnp.minimum(BINS - 1 - bins, SMOOTH) + 1
    inverse_count = 1.0 / count.astype(F32)
    for high in range(4):
        total = power[high, 4 + at : 4 + at + NB, :]
        for offset in range(5, 4 + 2 * SMOOTH + 1):
            total = total + power[high, at + offset : at + offset + NB, :]
        factor = valid[high] * lax.rsqrt(total * inverse_count + 0.1)
        for ri in range(2):
            row = part * PART_ROWS + (high * 2 + ri) * NB
            out[dst, row : row + NB, :] = (spec[ri, high, at : at + NB, :] * factor).astype(BF)


def spectra_kernel(rec_far, table_far, mask_far, out_far, out, mask, rec, rows, table, planes, spec, power, sems, out_sems):
    chunk = 4
    copies = [
        pltpu.make_async_copy(rec_far.at[c : c + chunk], rec.at[c : c + chunk], sems.at[c // chunk])
        for c in range(0, CH, chunk)
    ]
    mask_copy = pltpu.make_async_copy(mask_far, mask, sems.at[CH // chunk + PARTS])
    for copy in copies + [mask_copy]:
        copy.start()
    table_copies = [
        pltpu.make_async_copy(table_far.at[part], table.at[part], sems.at[CH // chunk + part])
        for part in range(PARTS)
    ]
    for copy in table_copies:
        copy.start()
    for c in range(0, CH, chunk):
        copies[c // chunk].wait()
        signal = rec[c : c + chunk].astype(F32).reshape(chunk * WIN, SEG)
        centred = signal - jnp.mean(signal, axis=-1, keepdims=True)
        spread = jnp.sqrt(jnp.mean(centred * centred, axis=-1, keepdims=True) + 1e-06)
        normal = centred * (1.0 / spread)
        for t in range(SEG // 128):
            for i in range(chunk):
                planes[t, (c + i) * STRIDE : (c + i) * STRIDE + WIN, :] = normal[i * WIN : (i + 1) * WIN, t * 128 : (t + 1) * 128]
    for w in range(WIN):
        for t in range(SEG // 128):
            rows[w * CH : (w + 1) * CH, t * 128 : (t + 1) * 128] = planes[
                t, pl.ds(w, CH, stride=STRIDE), :
            ].astype(BF)
    mask_copy.wait()
    valid = mask_lanes(mask[...])
    sent_mask = jnp.concatenate(valid + [jnp.zeros((4, 128), F32)], axis=0).astype(BF)
    for part in range(PARTS):
        table_copies[part].wait()
        multiply(rows, table.at[part], spec.at[part], power.at[part])
    out_copies = []
    for first in range(0, 16, 4):
        for dst in range(first, first + 4):
            for part in range(PARTS):
                whiten(part, dst, valid, out, spec.at[part], power.at[part])
            out[dst, MASK_ROW:SENT_ROWS, :] = sent_mask
        dsts = pl.ds(first, 4)
        out_copies.append(
            pltpu.make_async_copy(out.at[dsts], out_far.at[dsts], out_sems.at[first // 4])
        )
        out_copies[-1].start()
    for copy in out_copies:
        copy.wait()


def spectra(records, gap_mask):
    far = pl.BlockSpec(memory_space=pltpu.HBM)
    return pl.pallas_call(
        spectra_kernel,
        out_shape=jax.ShapeDtypeStruct((16, SENT_ROWS, 128), BF),
        in_specs=[far] * 3,
        out_specs=far,
        scratch_shapes=[
            pltpu.VMEM((16, SENT_ROWS, 128), BF),
            pltpu.VMEM((WIN, CH), jnp.int32),
            pltpu.VMEM((CH, WIN, SEG), BF),
            pltpu.VMEM((512, SEG), BF),
            pltpu.VMEM((PARTS, 2 * WIDE, SEG), BF),
            pltpu.VMEM((SEG // 128, CH * STRIDE + 32, 128), F32),
            pltpu.VMEM((PARTS, 2, 4, WIDE, 128), F32),
            pltpu.VMEM((PARTS, 4, WIDE + 16, 128), F32),
            pltpu.SemaphoreType.DMA((9 + PARTS,)),
            pltpu.SemaphoreType.DMA((4,)),
        ],
        compiler_params=pltpu.CompilerParams(vmem_limit_bytes=62 << 20),
        cost_estimate=pl.CostEstimate(
            flops=2 * 512 * SEG * 2 * BINS, bytes_accessed=8 << 20, transcendentals=0
        ),
        name="spectra",
    )(records, jnp.asarray(np.stack([forward_table(p) for p in range(PARTS)])), gap_mask.T)


def rolled(value, lanes):
    return pltpu.roll(value, lanes % 128, 1) if lanes % 128 else value


def blocks_to_lanes(parts):
    slot = lax.broadcasted_iota(jnp.int32, parts[0].shape, 1) // 32
    found = []
    for low in range(4):
        value = parts[-low % 4]
        for at in range(1, 4):
            value = jnp.where(slot == at, parts[(at - low) % 4], value)
        found.append(rolled(value, -32 * low))
    return found


def cross_kernel(part, own, prev, out_far, planes, pairs, out, sems):
    for block in range(7):
        for v in range(4):
            for ri in range(2):
                source, first = (
                    (prev.at[block * 4 + v], 0)
                    if block < 3
                    else (own.at[(block - 3) * 4 + v], part * PART_ROWS)
                )
                for high in range(4):
                    row = ((block * 2 + ri) * 4 + v) * 4 + high
                    at = first + (high * 2 + ri) * NB
                    value = source[at : at + NB, :].astype(F32)
                    planes[row * STRIDE : row * STRIDE + NB, :] = rolled(value, 32 * (block + 1 if block < 3 else block - 3))
    lane = lax.broadcasted_iota(jnp.int32, (32, 128), 1)

    def one_bin(k, carry):
        def side(blocks):
            found = []
            for ri in range(2):
                parts = [
                    planes[pl.ds((block * 2 + ri) * 16 * STRIDE + k, 16, stride=STRIDE), :] for block in blocks
                ]
                found.append(jnp.concatenate(blocks_to_lanes(parts), axis=0))
            return found

        prev_real, prev_imag = side((0, 0, 1, 2))
        own_real, own_imag = side((3, 4, 5, 6))
        left = jnp.concatenate(
            [
                jnp.concatenate([own_real, own_imag], axis=0),
                jnp.concatenate([own_imag, -own_real], axis=0),
            ],
            axis=1,
        ).astype(BF)
        right = jnp.concatenate(
            [
                jnp.concatenate([prev_real, prev_imag], axis=0),
                jnp.concatenate([own_real, own_imag], axis=0),
            ],
            axis=1,
        ).astype(BF)
        product = tn_dot(left, right)
        for ri in range(2):
            for b in range(4):
                at = ri * 128 + b * 32
                first, second = product[at : at + 32, :128], product[at : at + 32, 128:]
                value = jnp.where(lane < 32 * b + 32, second, first)
                pairs[pl.ds(at * STRIDE + k, 32, stride=STRIDE), :] = value
        return carry

    lax.fori_loop(0, NB, one_bin, 0, unroll=8)
    lanes = lax.broadcasted_iota(jnp.int32, (NB, 128), 1)
    copies = []
    for b in range(4):
        for ri in range(2):
            for v in range(4):
                for high in range(2):
                    row = ri * 128 + b * 32 + v * 8 + high * 4
                    p0, p1, p2, p3 = [pairs[(row + i) * STRIDE : (row + i) * STRIDE + NB, :] for i in range(4)]
                    first = 32 * b + 32
                    p0, p1 = rolled(p0, -first), rolled(p1, 96 - first)
                    p2, p3 = rolled(p2, 64 - first), rolled(p3, 32 - first)
                    target = out.at[b * 4 + v, ri, high]
                    target[:, 0:128] = jnp.where(lanes < 96, p0, p1).astype(BF)
                    target[:, 128:256] = jnp.where(lanes < 64, p1, p2).astype(BF)
                    target[:, 256:384] = jnp.where(lanes < 32, p2, p3).astype(BF)
        dsts = pl.ds(b * 4, 4)
        copies.append(pltpu.make_async_copy(out.at[dsts], out_far.at[dsts], sems.at[b]))
        copies[b].start()
    for copy in copies:
        copy.wait()


def cross(part, own, prev):
    full = pl.BlockSpec(memory_space=pltpu.VMEM)
    return pl.pallas_call(
        functools.partial(cross_kernel, part),
        out_shape=jax.ShapeDtypeStruct((16, 2, 2, NB, 384), BF),
        in_specs=[full] * 2,
        out_specs=pl.BlockSpec(memory_space=pltpu.HBM),
        scratch_shapes=[
            pltpu.VMEM((7 * 32 * STRIDE + 32, 128), F32),
            pltpu.VMEM((256 * STRIDE + 32, 128), F32),
            pltpu.VMEM((16, 2, 2, NB, 384), BF),
            pltpu.SemaphoreType.DMA((4,)),
        ],
        compiler_params=pltpu.CompilerParams(vmem_limit_bytes=48 << 20),
        cost_estimate=pl.CostEstimate(flops=CROSS_FLOPS[part], bytes_accessed=1 << 20, transcendentals=0),
        name="cross",
    )(own, prev)


def turned(value, ri, high):
    return value[:, ri, high].reshape(PART_BINS, 384).T


def turn_kernel(value, own_mask, partner_mask, table_far, out, scales, table, sem):
    copy = pltpu.make_async_copy(table_far, table, sem)
    copy.start()
    for ri in range(2):
        for high in range(2):
            out[ri, high * 384 : (high + 1) * 384, :] = turned(value, ri, high)
    count = nt_dot(partner_mask[...], own_mask[...])
    scale = 1.0 / jnp.sqrt(jnp.maximum(count, 1.0))
    for c in range(8):
        scales[c * 96 : (c + 1) * 96, :] = jnp.broadcast_to(scale[:, c : c + 1], (96, 128))
    copy.wait()


def turn(value, own_mask, partner_mask):
    near = pl.BlockSpec(memory_space=pltpu.VMEM)
    return pl.pallas_call(
        turn_kernel,
        out_shape=[
            jax.ShapeDtypeStruct((2, 768, PART_BINS), BF),
            jax.ShapeDtypeStruct((768, 128), F32),
            jax.ShapeDtypeStruct((BINS, 1024), BF),
        ],
        in_specs=[near] * 3 + [pl.BlockSpec(memory_space=pltpu.HBM)],
        out_specs=[near] * 3,
        scratch_shapes=[pltpu.SemaphoreType.DMA],
        compiler_params=pltpu.CompilerParams(vmem_limit_bytes=8 << 20),
        cost_estimate=pl.CostEstimate(flops=0, bytes_accessed=4 << 20, transcendentals=0),
        name="turn",
    )(value, own_mask, partner_mask, jnp.asarray(inverse_table()[0]))


def lag_kernel(first, second, scales, cosines, sines, out, left, back):
    for ri in range(2):
        left[ri, :, :PART_BINS] = first[ri]
        left[ri, :, PART_BINS:] = turned(second, ri, 0)
    row = lax.broadcasted_iota(jnp.int32, (256, 256), 0)
    col = lax.broadcasted_iota(jnp.int32, (256, 256), 1)
    reverse = ((row // 128 == col // 128) & ((row + col) % 128 == 80)).astype(BF)
    lane = lax.broadcasted_iota(jnp.int32, (CH, 128), 1)
    for at in (512, 0):
        even = jnp.dot(left[0], cosines[:, at : at + 512], preferred_element_type=F32)
        odd = jnp.dot(left[1], sines[:, at : at + 512], preferred_element_type=F32)
        ahead, behind = even + odd, even - odd
        for pair in range(2):
            both = []
            for tile in range(2):
                lanes = slice((pair * 2 + tile) * 128, (pair * 2 + tile + 1) * 128)
                both.append((ahead[:, lanes] * scales[...]).astype(BF))
            back[:, at + pair * 256 : at + pair * 256 + 256] = jnp.dot(
                jnp.concatenate(both, axis=1), reverse, preferred_element_type=F32
            )
        for low in range(4):
            for s in range(3):
                rows = slice(low * 96 + s * 32, low * 96 + s * 32 + 32)
                for tile in range(4):
                    lanes = slice(tile * 128, (tile + 1) * 128)
                    value = behind[rows, lanes] * scales[rows, :]
                    if at + tile * 128 == 896:
                        value = jnp.where(lane <= LAGHALF - 896, value, back[rows, 896:1024])
                    out[2 - s, low, :, at + tile * 128 : at + (tile + 1) * 128] = value.astype(BF)
    for low in range(4):
        for s in range(3):
            rows = slice(low * 96 + s * 32, low * 96 + s * 32 + 32)
            for tile in range(8):
                high_lanes = back[rows, (7 - tile) * 128 : (8 - tile) * 128]
                if tile < 7:
                    low_lanes = back[rows, (6 - tile) * 128 : (7 - tile) * 128]
                    value = jnp.where(lane <= 80, high_lanes, low_lanes)
                    out[2 - s, low, :, 1024 + tile * 128 : 1152 + tile * 128] = value.astype(BF)
                else:
                    out[2 - s, low, :, 1920:LAGS] = high_lanes[:, : LAGS - 1920].astype(BF)


def lag_sums(first, second, scales, cosines):
    return pl.pallas_call(
        lag_kernel,
        grid=(2,),
        out_shape=jax.ShapeDtypeStruct((3, 8, CH, LAGS), BF),
        in_specs=[
            pl.BlockSpec((2, 384, PART_BINS), lambda h: (0, h, 0)),
            pl.BlockSpec((16, 2, 1, NB, 384), lambda h: (0, 0, h, 0, 0)),
            pl.BlockSpec((384, 128), lambda h: (h, 0)),
            pl.BlockSpec((BINS, 1024), lambda h: (0, 0)),
            pl.BlockSpec((BINS, 1024), lambda h: (0, 0)),
        ],
        out_specs=pl.BlockSpec((3, 4, CH, LAGS), lambda h: (0, h, 0, 0)),
        scratch_shapes=[pltpu.VMEM((2, 384, BINS), BF), pltpu.VMEM((384, 1024), F32)],
        compiler_params=pltpu.CompilerParams(vmem_limit_bytes=59 << 20),
        cost_estimate=pl.CostEstimate(
            flops=768 * 2 * BINS * LAGS, bytes_accessed=7 << 20, transcendentals=0
        ),
        name="lag_sums",
    )(first, second, scales, cosines, jnp.asarray(inverse_table()[1]))


def shifted(value, axes, count, steps):
    return lax.ppermute(value, axes, [(i, (i + steps) % count) for i in range(count)])


def from_previous_group(value):
    return shifted(value, ("y", "zh"), 16, 1)


def per_device(records, gap_mask):
    own = lax.all_to_all(spectra(records, gap_mask), GROUP, 0, 0, tiled=True)
    prevs = [from_previous_group(own[4:, :PART_ROWS])]
    halo, prevs[0] = lax.optimization_barrier((own[4:, PART_ROWS:], prevs[0]))
    prevs.append(from_previous_group(halo))
    crosses = [
        lax.all_to_all(cross(p, own, prevs[p]), GROUP, 0, 0, tiled=True) for p in range(PARTS)
    ]
    masks = jnp.concatenate([prevs[-1][:, PART_ROWS : PART_ROWS + 4], own[:, MASK_ROW : MASK_ROW + 4]], axis=0)
    masks = lax.dynamic_slice_in_dim(masks, lax.axis_index("x") * 4, 16, 0)
    masks = masks.reshape(4, 16, 4, CH).transpose(0, 3, 1, 2).reshape(4 * CH, 64)
    own_mask = lax.dynamic_slice_in_dim(masks, 3 * CH + lax.axis_index(("zl", "core")) * 8, 8, 0)
    first, scales, cosines = turn(crosses[0], own_mask, masks[: 3 * CH])
    return lag_sums(first, crosses[1], scales, cosines)


def solution(mesh):
    fine = Mesh(mesh.devices.reshape(4, 4, 4, 2, 2), ("y", "zh", "x", "zl", "core"))
    in_specs = (P(("y", "zh", "x"), ("zl", "core"), None), P(("y", "zh", "x"), ("zl", "core")))
    out_specs = P(None, ("y", "zh", "x", "zl", "core"), None, None)
    return jax.shard_map(
        per_device, mesh=fine, in_specs=in_specs, out_specs=out_specs, check_vma=False
    )
```

```python
import functools
import math

import jax
import jax.numpy as jnp
import numpy as np
from jax import lax
from jax.experimental import pallas as pl
from jax.experimental.pallas import tpu as pltpu
from jax.sharding import Mesh, PartitionSpec as P

SEG = 2048
NFFT = 4096
BINS = 512
SMOOTH = 4
LAGHALF = 1000
LAGS = 2001
CH = 32
WIN = 16
BF = jnp.bfloat16
F32 = jnp.float32
PARTS = 2
PART_BINS = BINS // PARTS
NB = PART_BINS // 16
PART_ROWS = 8 * NB
STRIDE = NB + 1
MASK_ROW = PARTS * PART_ROWS
SENT_ROWS = MASK_ROW + 8
OWN_ROWS = SENT_ROWS
NEAR = 16
WIDE = PART_BINS + NEAR
CROSS_FLOPS = (0, 100 << 30)
GROUP = ("x", "zl", "core")
STATIONS = ("y", "zh", "x")


def forward_table(part):
    first = part * (PART_BINS - NEAR)
    phases = np.arange(first + 1, first + WIDE + 1)[:, None] * np.arange(SEG)[None, :] % NFFT
    angles = phases * (2.0 * math.pi / NFFT)
    table = np.concatenate([np.cos(angles), -np.sin(angles)], axis=0) / math.sqrt(SEG)
    return table.astype(np.float32).astype(jnp.bfloat16)


def inverse_table():
    phases = np.arange(1, BINS + 1)[:, None] * np.arange(LAGHALF, -1, -1)[None, :] % NFFT
    angles = phases * (2.0 * math.pi / NFFT)
    table = np.stack([np.cos(angles), -np.sin(angles)], axis=0) * math.sqrt(2.0 / BINS)
    return np.pad(table, ((0, 0), (0, 0), (0, 23))).astype(np.float32).astype(jnp.bfloat16)


def nt_dot(a, b):
    return lax.dot_general(a, b, (((1,), (1,)), ((), ())), preferred_element_type=F32)


def tn_dot(a, b):
    return lax.dot_general(a, b, (((0,), (0,)), ((), ())), preferred_element_type=F32)


def mask_lanes(mask):
    channel = lax.broadcasted_iota(jnp.int32, (CH, 512), 0)
    pick = (lax.broadcasted_iota(jnp.int32, (CH, 512), 1) % CH == channel).astype(BF)
    spread = jnp.dot(mask.astype(F32).astype(BF), pick, preferred_element_type=F32)
    window = lax.broadcasted_iota(jnp.int32, (WIN, 512), 0)
    own_lane = lax.broadcasted_iota(jnp.int32, (WIN, 512), 1) // CH == window
    valid = jnp.sum(jnp.where(own_lane, spread, 0.0), axis=0, keepdims=True)
    return [valid[:, i * 128 : (i + 1) * 128] for i in range(4)]


def multiply(rows, table, spec, power):
    for ri in range(2):
        value = nt_dot(table[ri * WIDE : (ri + 1) * WIDE, :], rows[...])
        for high in range(4):
            spec[ri, high] = value[:, high * 128 : (high + 1) * 128]
    for high in range(4):
        power[high, 0:8, :] = jnp.zeros((8, 128), F32)
        power[high, 8 + WIDE : 16 + WIDE, :] = jnp.zeros((8, 128), F32)
        real, imag = spec[0, high], spec[1, high]
        power[high, 8 : 8 + WIDE, :] = real * real + imag * imag


def whiten(part, dst, valid, out, spec, power):
    at = part * NEAR + dst * NB
    bins = part * PART_BINS + dst * NB + lax.broadcasted_iota(jnp.int32, (NB, 128), 0)
    count = jnp.minimum(bins, SMOOTH) + jnp.minimum(BINS - 1 - bins, SMOOTH) + 1
    inverse_count = 1.0 / count.astype(F32)
    for high in range(4):
        total = power[high, 4 + at : 4 + at + NB, :]
        for offset in range(5, 4 + 2 * SMOOTH + 1):
            total = total + power[high, at + offset : at + offset + NB, :]
        factor = valid[high] * lax.rsqrt(total * inverse_count + 0.1)
        for ri in range(2):
            row = part * PART_ROWS + (high * 2 + ri) * NB
            out[dst, row : row + NB, :] = (spec[ri, high, at : at + NB, :] * factor).astype(BF)


def spectra_kernel(rec_far, table_far, mask_far, out_far, out, mask, rec, rows, table, planes, spec, power, sems, out_sems):
    chunk = 8
    copies = [
        pltpu.make_async_copy(rec_far.at[c : c + chunk], rec.at[c : c + chunk], sems.at[c // chunk])
        for c in range(0, CH, chunk)
    ]
    mask_copy = pltpu.make_async_copy(mask_far, mask, sems.at[CH // chunk + PARTS])
    for copy in copies + [mask_copy]:
        copy.start()
    table_copies = [
        pltpu.make_async_copy(table_far.at[part], table.at[part], sems.at[CH // chunk + part])
        for part in range(PARTS)
    ]
    for copy in table_copies:
        copy.start()
    for c in range(0, CH, chunk):
        copies[c // chunk].wait()
        signal = rec[c : c + chunk].astype(F32).reshape(chunk * WIN, SEG)
        centred = signal - jnp.mean(signal, axis=-1, keepdims=True)
        spread = jnp.sqrt(jnp.mean(centred * centred, axis=-1, keepdims=True) + 1e-06)
        normal = centred * (1.0 / spread)
        for t in range(SEG // 128):
            for i in range(chunk):
                planes[t, (c + i) * STRIDE : (c + i) * STRIDE + WIN, :] = normal[i * WIN : (i + 1) * WIN, t * 128 : (t + 1) * 128]
    for w in range(WIN):
        for t in range(SEG // 128):
            rows[w * CH : (w + 1) * CH, t * 128 : (t + 1) * 128] = planes[
                t, pl.ds(w, CH, stride=STRIDE), :
            ].astype(BF)
    mask_copy.wait()
    valid = mask_lanes(mask[...])
    sent_mask = jnp.concatenate(valid + [jnp.zeros((4, 128), F32)], axis=0).astype(BF)
    for part in range(PARTS):
        table_copies[part].wait()
        multiply(rows, table.at[part], spec.at[part], power.at[part])
    out_copies = []
    for first in range(0, 16, 4):
        for dst in range(first, first + 4):
            for part in range(PARTS):
                whiten(part, dst, valid, out, spec.at[part], power.at[part])
            out[dst, MASK_ROW:SENT_ROWS, :] = sent_mask
        dsts = pl.ds(first, 4)
        out_copies.append(
            pltpu.make_async_copy(out.at[dsts], out_far.at[dsts], out_sems.at[first // 4])
        )
        out_copies[-1].start()
    for copy in out_copies:
        copy.wait()


def spectra(records, gap_mask):
    far = pl.BlockSpec(memory_space=pltpu.HBM)
    return pl.pallas_call(
        spectra_kernel,
        out_shape=jax.ShapeDtypeStruct((16, SENT_ROWS, 128), BF),
        in_specs=[far] * 3,
        out_specs=far,
        scratch_shapes=[
            pltpu.VMEM((16, SENT_ROWS, 128), BF),
            pltpu.VMEM((WIN, CH), jnp.int32),
            pltpu.VMEM((CH, WIN, SEG), BF),
            pltpu.VMEM((512, SEG), BF),
            pltpu.VMEM((PARTS, 2 * WIDE, SEG), BF),
            pltpu.VMEM((SEG // 128, CH * STRIDE + 32, 128), F32),
            pltpu.VMEM((PARTS, 2, 4, WIDE, 128), F32),
            pltpu.VMEM((PARTS, 4, WIDE + 16, 128), F32),
            pltpu.SemaphoreType.DMA((9 + PARTS,)),
            pltpu.SemaphoreType.DMA((4,)),
        ],
        compiler_params=pltpu.CompilerParams(vmem_limit_bytes=62 << 20),
        cost_estimate=pl.CostEstimate(
            flops=2 * 512 * SEG * 2 * BINS, bytes_accessed=8 << 20, transcendentals=0
        ),
        name="spectra",
    )(records, jnp.asarray(np.stack([forward_table(p) for p in range(PARTS)])), gap_mask.T)


def rolled(value, lanes):
    return pltpu.roll(value, lanes % 128, 1) if lanes % 128 else value


def blocks_to_lanes(parts):
    slot = lax.broadcasted_iota(jnp.int32, parts[0].shape, 1) // 32
    found = []
    for low in range(4):
        value = parts[-low % 4]
        for at in range(1, 4):
            value = jnp.where(slot == at, parts[(at - low) % 4], value)
        found.append(rolled(value, -32 * low))
    return found


def cross_kernel(part, own, prev, out_far, planes, pairs, out, sems):
    for block in range(7):
        for v in range(4):
            for ri in range(2):
                source, first = (
                    (prev.at[block * 4 + v], 0)
                    if block < 3
                    else (own.at[(block - 3) * 4 + v], part * PART_ROWS)
                )
                for high in range(4):
                    row = ((block * 2 + ri) * 4 + v) * 4 + high
                    at = first + (high * 2 + ri) * NB
                    value = source[at : at + NB, :].astype(F32)
                    planes[row * STRIDE : row * STRIDE + NB, :] = rolled(value, 32 * (block + 1 if block < 3 else block - 3))
    lane = lax.broadcasted_iota(jnp.int32, (32, 128), 1)

    def one_bin(k, carry):
        def side(blocks):
            found = []
            for ri in range(2):
                parts = [
                    planes[pl.ds((block * 2 + ri) * 16 * STRIDE + k, 16, stride=STRIDE), :] for block in blocks
                ]
                found.append(jnp.concatenate(blocks_to_lanes(parts), axis=0))
            return found

        prev_real, prev_imag = side((0, 0, 1, 2))
        own_real, own_imag = side((3, 4, 5, 6))
        left = jnp.concatenate(
            [
                jnp.concatenate([own_real, own_imag], axis=0),
                jnp.concatenate([own_imag, -own_real], axis=0),
            ],
            axis=1,
        ).astype(BF)
        right = jnp.concatenate(
            [
                jnp.concatenate([prev_real, prev_imag], axis=0),
                jnp.concatenate([own_real, own_imag], axis=0),
            ],
            axis=1,
        ).astype(BF)
        product = tn_dot(left, right)
        for ri in range(2):
            for b in range(4):
                at = ri * 128 + b * 32
                first, second = product[at : at + 32, :128], product[at : at + 32, 128:]
                value = jnp.where(lane < 32 * b + 32, second, first)
                pairs[pl.ds(at * STRIDE + k, 32, stride=STRIDE), :] = value
        return carry

    lax.fori_loop(0, NB, one_bin, 0, unroll=8)
    lanes = lax.broadcasted_iota(jnp.int32, (NB, 128), 1)
    copies = []
    for b in range(4):
        for ri in range(2):
            for v in range(4):
                for high in range(2):
                    row = ri * 128 + b * 32 + v * 8 + high * 4
                    p0, p1, p2, p3 = [pairs[(row + i) * STRIDE : (row + i) * STRIDE + NB, :] for i in range(4)]
                    first = 32 * b + 32
                    p0, p1 = rolled(p0, -first), rolled(p1, 96 - first)
                    p2, p3 = rolled(p2, 64 - first), rolled(p3, 32 - first)
                    target = out.at[b * 4 + v, ri, high]
                    target[:, 0:128] = jnp.where(lanes < 96, p0, p1).astype(BF)
                    target[:, 128:256] = jnp.where(lanes < 64, p1, p2).astype(BF)
                    target[:, 256:384] = jnp.where(lanes < 32, p2, p3).astype(BF)
        dsts = pl.ds(b * 4, 4)
        copies.append(pltpu.make_async_copy(out.at[dsts], out_far.at[dsts], sems.at[b]))
        copies[b].start()
    for copy in copies:
        copy.wait()


def cross(part, own, prev):
    full = pl.BlockSpec(memory_space=pltpu.VMEM)
    return pl.pallas_call(
        functools.partial(cross_kernel, part),
        out_shape=jax.ShapeDtypeStruct((16, 2, 2, NB, 384), BF),
        in_specs=[full] * 2,
        out_specs=pl.BlockSpec(memory_space=pltpu.HBM),
        scratch_shapes=[
            pltpu.VMEM((7 * 32 * STRIDE + 32, 128), F32),
            pltpu.VMEM((256 * STRIDE + 32, 128), F32),
            pltpu.VMEM((16, 2, 2, NB, 384), BF),
            pltpu.SemaphoreType.DMA((4,)),
        ],
        compiler_params=pltpu.CompilerParams(vmem_limit_bytes=48 << 20),
        cost_estimate=pl.CostEstimate(flops=CROSS_FLOPS[part], bytes_accessed=1 << 20, transcendentals=0),
        name="cross",
    )(own, prev)


def turned(value, ri, high):
    return value[:, ri, high].reshape(PART_BINS, 384).T


def turn_kernel(value, own_mask, partner_mask, table_far, out, scales, table, sem):
    copy = pltpu.make_async_copy(table_far, table, sem)
    copy.start()
    for ri in range(2):
        for high in range(2):
            out[ri, high * 384 : (high + 1) * 384, :] = turned(value, ri, high)
    count = nt_dot(partner_mask[...], own_mask[...])
    scale = 1.0 / jnp.sqrt(jnp.maximum(count, 1.0))
    for c in range(8):
        scales[c * 96 : (c + 1) * 96, :] = jnp.broadcast_to(scale[:, c : c + 1], (96, 128))
    copy.wait()


def turn(value, own_mask, partner_mask):
    near = pl.BlockSpec(memory_space=pltpu.VMEM)
    return pl.pallas_call(
        turn_kernel,
        out_shape=[
            jax.ShapeDtypeStruct((2, 768, PART_BINS), BF),
            jax.ShapeDtypeStruct((768, 128), F32),
            jax.ShapeDtypeStruct((BINS, 1024), BF),
        ],
        in_specs=[near] * 3 + [pl.BlockSpec(memory_space=pltpu.HBM)],
        out_specs=[near] * 3,
        scratch_shapes=[pltpu.SemaphoreType.DMA],
        compiler_params=pltpu.CompilerParams(vmem_limit_bytes=8 << 20),
        cost_estimate=pl.CostEstimate(flops=0, bytes_accessed=4 << 20, transcendentals=0),
        name="turn",
    )(value, own_mask, partner_mask, jnp.asarray(inverse_table()[0]))


def lag_kernel(first, second, scales, cosines, sines, out, left, back):
    for ri in range(2):
        left[ri, :, :PART_BINS] = first[ri]
        left[ri, :, PART_BINS:] = turned(second, ri, 0)
    row = lax.broadcasted_iota(jnp.int32, (256, 256), 0)
    col = lax.broadcasted_iota(jnp.int32, (256, 256), 1)
    reverse = ((row // 128 == col // 128) & ((row + col) % 128 == 80)).astype(BF)
    lane = lax.broadcasted_iota(jnp.int32, (CH, 128), 1)
    for at in (512, 0):
        even = jnp.dot(left[0], cosines[:, at : at + 512], preferred_element_type=F32)
        odd = jnp.dot(left[1], sines[:, at : at + 512], preferred_element_type=F32)
        ahead, behind = even + odd, even - odd
        for pair in range(2):
            both = []
            for tile in range(2):
                lanes = slice((pair * 2 + tile) * 128, (pair * 2 + tile + 1) * 128)
                both.append((ahead[:, lanes] * scales[...]).astype(BF))
            back[:, at + pair * 256 : at + pair * 256 + 256] = jnp.dot(
                jnp.concatenate(both, axis=1), reverse, preferred_element_type=F32
            )
        for low in range(4):
            for s in range(3):
                rows = slice(low * 96 + s * 32, low * 96 + s * 32 + 32)
                for tile in range(4):
                    lanes = slice(tile * 128, (tile + 1) * 128)
                    value = behind[rows, lanes] * scales[rows, :]
                    if at + tile * 128 == 896:
                        value = jnp.where(lane <= LAGHALF - 896, value, back[rows, 896:1024])
                    out[2 - s, low, :, at + tile * 128 : at + (tile + 1) * 128] = value.astype(BF)
    for low in range(4):
        for s in range(3):
            rows = slice(low * 96 + s * 32, low * 96 + s * 32 + 32)
            for tile in range(8):
                high_lanes = back[rows, (7 - tile) * 128 : (8 - tile) * 128]
                if tile < 7:
                    low_lanes = back[rows, (6 - tile) * 128 : (7 - tile) * 128]
                    value = jnp.where(lane <= 80, high_lanes, low_lanes)
                    out[2 - s, low, :, 1024 + tile * 128 : 1152 + tile * 128] = value.astype(BF)
                else:
                    out[2 - s, low, :, 1920:LAGS] = high_lanes[:, : LAGS - 1920].astype(BF)


def lag_sums(first, second, scales, cosines):
    return pl.pallas_call(
        lag_kernel,
        grid=(2,),
        out_shape=jax.ShapeDtypeStruct((3, 8, CH, LAGS), BF),
        in_specs=[
            pl.BlockSpec((2, 384, PART_BINS), lambda h: (0, h, 0)),
            pl.BlockSpec((16, 2, 1, NB, 384), lambda h: (0, 0, h, 0, 0)),
            pl.BlockSpec((384, 128), lambda h: (h, 0)),
            pl.BlockSpec((BINS, 1024), lambda h: (0, 0)),
            pl.BlockSpec((BINS, 1024), lambda h: (0, 0)),
        ],
        out_specs=pl.BlockSpec((3, 4, CH, LAGS), lambda h: (0, h, 0, 0)),
        scratch_shapes=[pltpu.VMEM((2, 384, BINS), BF), pltpu.VMEM((384, 1024), F32)],
        compiler_params=pltpu.CompilerParams(vmem_limit_bytes=59 << 20),
        cost_estimate=pl.CostEstimate(
            flops=768 * 2 * BINS * LAGS, bytes_accessed=7 << 20, transcendentals=0
        ),
        name="lag_sums",
    )(first, second, scales, cosines, jnp.asarray(inverse_table()[1]))


def shifted(value, axes, count, steps):
    return lax.ppermute(value, axes, [(i, (i + steps) % count) for i in range(count)])


def from_previous_group(value):
    return shifted(value, ("y", "zh"), 16, 1)


def per_device(records, gap_mask):
    own = lax.all_to_all(spectra(records, gap_mask), GROUP, 0, 0, tiled=True)
    prevs = [from_previous_group(own[4:, :PART_ROWS])]
    halo, prevs[0] = lax.optimization_barrier((own[4:, PART_ROWS:], prevs[0]))
    prevs.append(from_previous_group(halo))
    crosses = [
        lax.all_to_all(cross(p, own, prevs[p]), GROUP, 0, 0, tiled=True) for p in range(PARTS)
    ]
    masks = jnp.concatenate([prevs[-1][:, PART_ROWS : PART_ROWS + 4], own[:, MASK_ROW : MASK_ROW + 4]], axis=0)
    masks = lax.dynamic_slice_in_dim(masks, lax.axis_index("x") * 4, 16, 0)
    masks = masks.reshape(4, 16, 4, CH).transpose(0, 3, 1, 2).reshape(4 * CH, 64)
    own_mask = lax.dynamic_slice_in_dim(masks, 3 * CH + lax.axis_index(("zl", "core")) * 8, 8, 0)
    first, scales, cosines = turn(crosses[0], own_mask, masks[: 3 * CH])
    return lag_sums(first, crosses[1], scales, cosines)


def solution(mesh):
    fine = Mesh(mesh.devices.reshape(4, 4, 4, 2, 2), ("y", "zh", "x", "zl", "core"))
    in_specs = (P(("y", "zh", "x"), ("zl", "core"), None), P(("y", "zh", "x"), ("zl", "core")))
    out_specs = P(None, ("y", "zh", "x", "zl", "core"), None, None)
    return jax.shard_map(
        per_device, mesh=fine, in_specs=in_specs, out_specs=out_specs, check_vma=False
    )
```
